128 devices in a mesh: ta: 16 (over y_hi, x, core), gz: 8 (over z, y_lo).
Axes of the slice: x: 4, y: 4 (y_hi: 2, y_lo: 2; y = y_hi * 2 + y_lo), z: 4, core: 2. Of those that a mesh axis runs over, the one named last changes fastest.
Arguments:
- gauge_links: float32 [4, 2, 3, 3, 16, 64, 1024], P(None, None, None, None, 'ta', 'gz'), may hold values from -1 to 1, as said below
Outputs:
- rotated: float32 [4, 2, 3, 3, 16, 64, 1024], P(None, None, None, None, 'ta', 'gz')
The draws below stay inside these ranges and needn't reach their ends.
Inputs may be any that keep to these rules, and one draw needn't show every extreme that they name: `gauge_links`: every link is a special unitary 3x3 matrix.
All inputs are finite; a program needn't handle non-finite values.
Results may differ from the reference program's by a relative error of at most 0.0001.
Values sent between devices are 32-bit elements; how exact they have to be, the bound alone decides.
A program may use at most 192 MiB of HBM per device.

```python
import jax
import jax.numpy as jnp
from jax import lax

LX = 32
LY = 32
ITERS = 2
LZ = 64
LT = 16


def matrix_product_drawn(left_real, left_imag, right_real, right_imag):
    out_real = []
    out_imag = []
    for row_index in range(3):
        real_row = []
        imag_row = []
        for column in range(3):
            total_real = left_real[row_index, 0] * right_real[0, column] - left_imag[row_index, 0] * right_imag[0, column]
            total_imag = left_real[row_index, 0] * right_imag[0, column] + left_imag[row_index, 0] * right_real[0, column]
            for inner_index in (1, 2):
                total_real = total_real + left_real[row_index, inner_index] * right_real[inner_index, column] - left_imag[row_index, inner_index] * right_imag[inner_index, column]
                total_imag = total_imag + left_real[row_index, inner_index] * right_imag[inner_index, column] + left_imag[row_index, inner_index] * right_real[inner_index, column]
            real_row.append(total_real)
            imag_row.append(total_imag)
        out_real.append(jnp.stack(real_row))
        out_imag.append(jnp.stack(imag_row))
    return (jnp.stack(out_real), jnp.stack(out_imag))


def subgroup_rotation(key, row_first, row_second, layout):
    subkeys = jax.random.split(key, 3)
    polar = jax.random.uniform(subkeys[0], layout, jnp.float32, 0.0, 0.5 * jnp.pi)
    phase_diagonal = jax.random.uniform(subkeys[1], layout, jnp.float32, -jnp.pi, jnp.pi)
    phase_offdiag = jax.random.uniform(subkeys[2], layout, jnp.float32, -jnp.pi, jnp.pi)
    cosine = jnp.cos(polar)
    sine_value = jnp.sin(polar)
    zeros_block = jnp.zeros(layout, jnp.float32)
    ones_block = jnp.ones(layout, jnp.float32)
    real_rows = [[ones_block if r == c else zeros_block for c in range(3)] for r in range(3)]
    imag_rows = [[zeros_block for c in range(3)] for r in range(3)]
    real_rows[row_first][row_first] = cosine * jnp.cos(phase_diagonal)
    imag_rows[row_first][row_first] = cosine * jnp.sin(phase_diagonal)
    real_rows[row_second][row_second] = cosine * jnp.cos(phase_diagonal)
    imag_rows[row_second][row_second] = -cosine * jnp.sin(phase_diagonal)
    real_rows[row_first][row_second] = sine_value * jnp.cos(phase_offdiag)
    imag_rows[row_first][row_second] = sine_value * jnp.sin(phase_offdiag)
    real_rows[row_second][row_first] = -sine_value * jnp.cos(phase_offdiag)
    imag_rows[row_second][row_first] = sine_value * jnp.sin(phase_offdiag)
    matrix_real = jnp.stack([jnp.stack(entry_row) for entry_row in real_rows])
    matrix_imag = jnp.stack([jnp.stack(entry_row) for entry_row in imag_rows])
    return (matrix_real, matrix_imag)


def draw_gauge_links(key, part):
    key = jax.random.fold_in(key, 11)
    layout = (4, LT, LZ, LX * LY)
    subkeys = jax.random.split(key, 3)
    first_real, first_imag = subgroup_rotation(subkeys[0], 0, 1, layout)
    second_real, second_imag = subgroup_rotation(subkeys[1], 1, 2, layout)
    third_real, third_imag = subgroup_rotation(subkeys[2], 0, 2, layout)
    product_real, product_imag = matrix_product_drawn(first_real, first_imag, second_real, second_imag)
    product_real, product_imag = matrix_product_drawn(product_real, product_imag, third_real, third_imag)
    link_field = jnp.stack([product_real, product_imag])
    return jnp.transpose(link_field, (3, 0, 1, 2, 4, 5, 6))


def setup_inputs(seed: int = 0) -> dict:
    seeds = jax.random.split(jax.random.key(seed), 2)
    return {
        "gauge_links": draw_gauge_links(jax.random.fold_in(seeds[1], 71), 0),
    }


def matrix_product(left_real, left_imag, right_real, right_imag):
    out_real = []
    out_imag = []
    for row_index in range(3):
        real_row = []
        imag_row = []
        for column in range(3):
            total_real = left_real[row_index, 0] * right_real[0, column] - left_imag[row_index, 0] * right_imag[0, column]
            total_imag = left_real[row_index, 0] * right_imag[0, column] + left_imag[row_index, 0] * right_real[0, column]
            for inner_index in (1, 2):
                total_real = total_real + left_real[row_index, inner_index] * right_real[inner_index, column] - left_imag[row_index, inner_index] * right_imag[inner_index, column]
                total_imag = total_imag + left_real[row_index, inner_index] * right_imag[inner_index, column] + left_imag[row_index, inner_index] * right_real[inner_index, column]
            real_row.append(total_real)
            imag_row.append(total_imag)
        out_real.append(jnp.stack(real_row))
        out_imag.append(jnp.stack(imag_row))
    return (jnp.stack(out_real), jnp.stack(out_imag))

def adjoint(matrix_real, matrix_imag):
    return (jnp.swapaxes(matrix_real, 0, 1), -jnp.swapaxes(matrix_imag, 0, 1))

def identity_like(matrix_real):
    return jnp.eye(3, dtype=jnp.float32).reshape((3, 3) + (1,) * (matrix_real.ndim - 2))

def antihermitian(w_real, w_imag):
    part_real = 0.5 * (w_real - jnp.swapaxes(w_real, 0, 1))
    part_imag = 0.5 * (w_imag + jnp.swapaxes(w_imag, 0, 1))
    trace_third = (w_imag[0, 0] + w_imag[1, 1] + w_imag[2, 2]) / 3.0
    return (part_real, part_imag - identity_like(w_real) * trace_third[None, None])

def normalized(row_real, row_imag):
    factor = 1.0 / jnp.sqrt(lax.optimization_barrier(jnp.sum(row_real * row_real + row_imag * row_imag, axis=0)))
    return (row_real * factor, row_imag * factor)

def unitary_projection(power_real, power_imag):
    first_real, first_imag = normalized(power_real[0], power_imag[0])
    proj_real = lax.optimization_barrier(jnp.sum(first_real * power_real[1] + first_imag * power_imag[1], axis=0))
    proj_imag = lax.optimization_barrier(jnp.sum(first_real * power_imag[1] - first_imag * power_real[1], axis=0))
    second_real = power_real[1] - (proj_real * first_real - proj_imag * first_imag)
    second_imag = power_imag[1] - (proj_real * first_imag + proj_imag * first_real)
    second_real, second_imag = normalized(second_real, second_imag)
    third_real = []
    third_imag = []
    for position in range(3):
        follow = (position + 1) % 3
        beyond = (position + 2) % 3
        cross_real = first_real[follow] * second_real[beyond] - first_imag[follow] * second_imag[beyond] - (first_real[beyond] * second_real[follow] - first_imag[beyond] * second_imag[follow])
        cross_imag = first_real[follow] * second_imag[beyond] + first_imag[follow] * second_real[beyond] - (first_real[beyond] * second_imag[follow] + first_imag[beyond] * second_real[follow])
        third_real.append(cross_real)
        third_imag.append(-cross_imag)
    gauge_real = jnp.stack([first_real, second_real, jnp.stack(third_real)])
    gauge_imag = jnp.stack([first_imag, second_imag, jnp.stack(third_imag)])
    return (gauge_real, gauge_imag)

def second_order_exponential(smooth_real, smooth_imag):
    exponent_real = 0.04 * smooth_real
    exponent_imag = 0.04 * smooth_imag
    square_real, square_imag = matrix_product(exponent_real, exponent_imag, exponent_real, exponent_imag)
    power_real = identity_like(smooth_real) + exponent_real + 0.5 * square_real
    power_imag = exponent_imag + 0.5 * square_imag
    return unitary_projection(power_real, power_imag)

def rotate_link(left_side, link_now, right_side):
    product_real, product_imag = matrix_product(left_side[0], left_side[1], link_now[0], link_now[1])
    adjoint_real, adjoint_imag = adjoint(right_side[0], right_side[1])
    new_real, new_imag = matrix_product(product_real, product_imag, adjoint_real, adjoint_imag)
    return jnp.stack([new_real, new_imag])

def displace(array, direction, amount):
    if direction == 3:
        return jnp.roll(array, amount, axis=-3)
    if direction == 2:
        return jnp.roll(array, amount, axis=-2)
    plane_grid = array.reshape(array.shape[:-1] + (LY, LX))
    shifted = jnp.roll(plane_grid, amount, axis=-1 if direction == 0 else -2)
    return shifted.reshape(array.shape)

def lattice_sine(mode_index, length):
    sine_value = jnp.sin(jnp.pi * mode_index.astype(jnp.float32) / length)
    return 4.0 * sine_value * sine_value

def filter_weight(time_length, depth_length):
    time_modes = jnp.arange(time_length, dtype=jnp.int32)[:, None, None, None]
    depth_modes = jnp.arange(depth_length, dtype=jnp.int32)[None, :, None, None]
    wave_y = jnp.arange(LY, dtype=jnp.int32)[None, None, :, None]
    wave_x = jnp.arange(LX, dtype=jnp.int32)[None, None, None, :]
    summed = lattice_sine(time_modes, time_length) + lattice_sine(depth_modes, depth_length) + lattice_sine(wave_y, LY) + lattice_sine(wave_x, LX)
    anchor = (time_modes == 0) & (depth_modes == 0) & (wave_y == 0) & (wave_x == 0)
    return jnp.where(anchor, 0.0, 16.0 / jnp.where(anchor, 1.0, summed))

def smooth_field(delta_real, delta_imag, weight):
    layout = delta_real.shape
    entries = (delta_real + 1j * delta_imag).reshape((9,) + layout[2:4] + (LY, LX))
    spectrum = jnp.fft.fftn(entries, axes=(1, 2, 3, 4))
    smooth = jnp.fft.ifftn(spectrum * weight[None], axes=(1, 2, 3, 4))
    return (jnp.real(smooth).reshape(layout), jnp.imag(smooth).reshape(layout))

def divergence(lattice):
    summed = jnp.zeros(lattice.shape[1:], jnp.float32)
    for direction in range(4):
        link_now = lattice[direction]
        summed = summed + displace(link_now, direction, 1) - link_now
    return (summed[0], summed[1])

def reference(gauge_links):
    lattice = gauge_links
    weight = filter_weight(lattice.shape[4], lattice.shape[5])
    for iteration in range(ITERS):
        summed_real, summed_imag = divergence(lattice)
        delta_real, delta_imag = antihermitian(summed_real, summed_imag)
        smooth_real, smooth_imag = smooth_field(delta_real, delta_imag, weight)
        gauge_real, gauge_imag = second_order_exponential(smooth_real, smooth_imag)
        gauge = jnp.stack([gauge_real, gauge_imag])
        rotated = []
        for direction in range(4):
            forward = displace(gauge, direction, -1)
            rotated.append(rotate_link(gauge, lattice[direction], forward))
        lattice = jnp.stack(rotated)
    return lattice
```

```python
import functools

import jax
import jax.numpy as jnp
import ml_dtypes
import numpy as np
from jax import lax
from jax.experimental import pallas as pl
from jax.experimental.pallas import tpu as pltpu
from jax.sharding import PartitionSpec as P

LX = 32
LY = 32
LZ = 64
LT = 16
ITERS = 2
NTA = 16
NGZ = 8
DEVICES = NTA * NGZ
MESH = pl.DeviceIdType.MESH
F32 = jnp.float32
BF16 = jnp.bfloat16


def cas(angle):
    return np.cos(angle) + np.sin(angle)


def halves(table):
    high = table.astype(ml_dtypes.bfloat16)
    low = (table - high.astype(np.float64)).astype(ml_dtypes.bfloat16)
    return high, low


def plane_modes():
    wave_y = [k for k in range(LY) if k % 4 == 0]
    wave_y += [k for k in range(LY) if k % 4 == 2]
    wave_y += [k for k in range(LY) if k % 2 == 1]
    return np.repeat(np.array(wave_y), LX), np.tile(np.arange(LX), LY)


def plane_tables():
    ky, kx = plane_modes()
    b = np.repeat(np.arange(8), LX)
    x = np.tile(np.arange(LX), 8)
    along_x = cas(2 * np.pi * (kx[:, None] * x[None, :] % LX) / LX)
    phase = 2 * np.pi * (ky[:, None] * b[None, :] % LY) / LY
    plain = cas(phase) * along_x
    sign = np.where(ky % 4 == 1, 1.0, -1.0)[:, None]
    mirrored = sign * cas(-phase) * along_x
    even = plain[0:512]
    odd = np.concatenate([plain[512:], mirrored[512:]], axis=1)
    return halves(even) + halves(odd)


def line_tables():
    t = np.arange(LT)
    along_t = cas(2 * np.pi * (t[:, None] * t[None, :] % LT) / LT)
    zb = np.arange(8)
    waves = [np.cos(0 * zb), np.cos(np.pi * zb)]
    for k in (1, 2, 3):
        waves += [np.cos(2 * np.pi * k * zb / 8), np.sin(2 * np.pi * k * zb / 8)]
    waves = np.stack(waves)
    first = np.einsum("qz,kt->qktz", waves, along_t).reshape(128, 128)
    z8 = np.arange(8)
    second = np.zeros((4, 2, 2, 8, 8, 8, 16))
    depth = np.zeros((4, 16), np.int64)
    for pair in range(4):
        for j in range(16):
            k1 = (0, 4)[j // 8] if pair == 0 else (pair, 8 - pair)[j // 8]
            kz = k1 + 8 * (j % 8)
            depth[pair, j] = kz
            beta = 2 * np.pi * (kz * z8 % LZ) / LZ
            for f in range(8):
                for s in range(2):
                    if pair == 0:
                        second[pair, j // 8, s, f, :, f, j] = cas(beta)
                    else:
                        second[pair, 0, s, f, :, f, j] = cas(beta)
                        second[pair, 1, s, f, :, f, j] = (1.0 if j < 8 else -1.0) * cas(-beta)
    second = second.reshape(4, 256, 128)
    sine_t = 4 * np.sin(np.pi * t / LT) ** 2
    sine_z = 4 * np.sin(np.pi * depth / LZ) ** 2
    base = np.zeros((4, 8, 16, 8, 16))
    base += sine_t[None, None, :, None, None] + sine_z[:, None, None, None, :]
    return first, second, base.reshape(4, 128, 128).astype(np.float32)


def make_tables():
    even_hi, even_lo, odd_hi, odd_lo = plane_tables()
    first, second, base = line_tables()
    first_hi, first_lo = halves(first)
    back_hi, back_lo = halves(first.T)
    second_hi, second_lo = halves(second)
    turned_hi, turned_lo = halves(np.swapaxes(second, 1, 2))
    firsts = np.stack(
        [
            np.concatenate([first_hi, first_hi], axis=1),
            np.concatenate([first_lo, np.zeros_like(first_lo)], axis=1),
            np.concatenate([back_hi, back_hi], axis=1),
            np.concatenate([back_lo, np.zeros_like(back_lo)], axis=1),
        ]
    )
    seconds = np.concatenate([second_hi, second_lo], axis=2)
    turned = np.concatenate([turned_hi, turned_lo], axis=1)
    ky, kx = plane_modes()
    sine_xy = 4 * np.sin(np.pi * ky / LY) ** 2 + 4 * np.sin(np.pi * kx / LX) ** 2
    sine_xy = np.repeat(sine_xy[:, None], 128, axis=1).astype(np.float32)
    return even_hi, even_lo, odd_hi, odd_lo, firsts, seconds, turned, base, sine_xy


def split(value):
    high = value.astype(BF16)
    return high, (value - high.astype(F32)).astype(BF16)


def fields_of(link):
    imag_sum = link(1, 0, 0) + link(1, 1, 1) + link(1, 2, 2)
    third = imag_sum * (2.0 / 3.0)
    return [
        link(0, 0, 1) - link(0, 1, 0),
        link(1, 0, 1) + link(1, 1, 0),
        link(0, 0, 2) - link(0, 2, 0),
        link(1, 0, 2) + link(1, 2, 0),
        link(0, 1, 2) - link(0, 2, 1),
        link(1, 1, 2) + link(1, 2, 1),
        2.0 * link(1, 0, 0) - third,
        2.0 * link(1, 1, 1) - third,
    ]


def inverse_root(value):
    guess = lax.rsqrt(value)
    return guess * (1.5 - 0.5 * value * guess * guess)


def cross_row(first, second):
    out = []
    for position in range(3):
        follow, beyond = (position + 1) % 3, (position + 2) % 3
        fr, fi = first[follow]
        gr, gi = first[beyond]
        sr, si = second[beyond]
        tr, ti = second[follow]
        real = fr * sr - fi * si - (gr * tr - gi * ti)
        imag = gr * ti + gi * tr - (fr * si + fi * sr)
        out.append((real, imag))
    return out


def gauge_of(x):
    a, b, c, d, e, f, d0, d1 = x
    n01 = a * a + b * b
    n02 = c * c + d * d
    n12 = e * e + f * f
    both = d0 + d1
    s01r = -both * b - (c * e + d * f)
    s01i = both * a - (d * e - c * f)
    s02r = d1 * d + (a * e - b * f)
    s02i = (a * f + b * e) - d1 * c
    s12r = d0 * f - (a * c + b * d)
    s12i = (b * c - a * d) - d0 * e
    r0 = [(1.0 - 0.5 * (d0 * d0 + n01 + n02), d0), (a + 0.5 * s01r, b + 0.5 * s01i), (c + 0.5 * s02r, d + 0.5 * s02i)]
    r1 = [(0.5 * s01r - a, b - 0.5 * s01i), (1.0 - 0.5 * (d1 * d1 + n01 + n12), d1), (e + 0.5 * s12r, f + 0.5 * s12i)]

    def unit(row):
        total = None
        for real, imag in row:
            term = real * real + imag * imag
            total = term if total is None else total + term
        scale = inverse_root(total)
        return [(real * scale, imag * scale) for real, imag in row]

    u0 = unit(r0)
    pr = pi = None
    for (ur, ui), (vr, vi) in zip(u0, r1):
        tr, ti = ur * vr + ui * vi, ur * vi - ui * vr
        pr = tr if pr is None else pr + tr
        pi = ti if pi is None else pi + ti
    v = [(vr - (pr * ur - pi * ui), vi - (pr * ui + pi * ur)) for (ur, ui), (vr, vi) in zip(u0, r1)]
    u1 = unit(v)
    return [u0, u1, cross_row(u0, u1)]


def rotated_link(left, link, right):
    rows = []
    for i in range(2):
        product = []
        for k in range(3):
            real = imag = None
            for m in range(3):
                lr, li = left[i][m]
                ur, ui = link(0, m, k), link(1, m, k)
                tr, ti = lr * ur - li * ui, lr * ui + li * ur
                real = tr if real is None else real + tr
                imag = ti if imag is None else imag + ti
            product.append((real, imag))
        row = []
        for j in range(3):
            real = imag = None
            for k in range(3):
                pr, pi = product[k]
                gr, gi = right[j][k]
                tr, ti = pr * gr + pi * gi, pi * gr - pr * gi
                real = tr if real is None else real + tr
                imag = ti if imag is None else imag + ti
            row.append((real, imag))
        rows.append(row)
    rows.append(cross_row(rows[0], rows[1]))
    return rows


def hop_count(offset):
    return sum(min(v, 4 - v) for v in offset[:3]) + 0.1 * offset[3]


OFFSETS = sorted(
    [
        (dx, dy, dz, dc)
        for dy in range(4)
        for dz in range(4)
        for dx in range(4)
        for dc in range(2)
        if dx + dy + dz + dc > 0
    ],
    key=lambda o: -hop_count(o),
)


def target(offset):
    ta = lax.axis_index("ta")
    gz = lax.axis_index("gz")
    y = (2 * (ta // 8) + gz % 2 + offset[1]) % 4
    to_ta = (y // 2) * 8 + (((ta // 2) % 4 + offset[0]) % 4) * 2 + (ta % 2 + offset[3]) % 2
    to_gz = ((gz // 2 + offset[2]) % 4) * 2 + y % 2
    return to_ta, to_gz


def kernel(
    links_hbm,
    even_hi_hbm,
    even_lo_hbm,
    odd_hi_hbm,
    odd_lo_hbm,
    firsts_hbm,
    seconds_hbm,
    turned_hbm,
    base_hbm,
    sine_hbm,
    out_hbm,
    links,
    even_hi,
    even_lo,
    odd_hi,
    odd_lo,
    firsts,
    seconds,
    turned,
    weight,
    sine,
    delta,
    along_y,
    along_z,
    exchange,
    smooth,
    gauge,
    ahead,
    link_out,
    link_in,
    edge_out,
    edge_in,
    table_sem,
    load_sem,
    store_sem,
    send_sem,
    recv_sem,
    edge_send_sem,
    edge_recv_sem,
):
    ta = lax.axis_index("ta")
    gz = lax.axis_index("gz")
    me = ta * NGZ + gz
    after = {"gz": (gz + 1) % NGZ}
    before = {"gz": (gz + NGZ - 1) % NGZ}

    barrier = pltpu.get_barrier_semaphore()
    loads = []
    for mu in (1, 0, 3, 2):
        for ct in range(8):
            copy = pltpu.make_async_copy(
                links_hbm.at[mu, :, :, :, 0, :, pl.ds(ct * 128, 128)],
                links.at[mu, :, :, :, pl.ds(ct * 8, 8), :],
                load_sem.at[mu],
            )
            copy.start()
    tables = []
    pairs = [
        (even_hi_hbm, even_hi),
        (even_lo_hbm, even_lo),
        (odd_hi_hbm, odd_hi),
        (odd_lo_hbm, odd_lo),
        (firsts_hbm, firsts),
        (seconds_hbm, seconds),
        (turned_hbm, turned),
        (base_hbm, weight),
        (sine_hbm.at[pl.ds(pl.multiple_of(me * 8, 8), 8)], sine),
    ]
    for index, (source, place) in enumerate(pairs):
        copy = pltpu.make_async_copy(source, place, table_sem.at[index])
        copy.start()
        tables.append(copy)
    for offset in OFFSETS:
        to_ta, to_gz = target(offset)
        pl.semaphore_signal(barrier, inc=1, device_id={"ta": to_ta, "gz": to_gz}, device_id_type=MESH)

    lane = lax.broadcasted_iota(jnp.int32, (8, 128), 1)
    first_x = lane % LX == 0
    last_x = lane % LX == LX - 1
    low_96 = lane < 96
    low_32 = lane < 32

    def tile_of(ref, mu, row):
        def link(part, i, k):
            return ref[mu, part, i, k, pl.ds(row, 8), :]

        return link

    def before_x(tile):
        return jnp.where(first_x, pltpu.roll(tile, 97, 1), pltpu.roll(tile, 1, 1))

    def after_x(tile):
        return jnp.where(last_x, pltpu.roll(tile, 31, 1), pltpu.roll(tile, 127, 1))

    def row_of(ct):
        return pl.multiple_of(ct * 8, 8)

    def wide_row(ct):
        return pl.multiple_of(ct * 16, 16)

    def load_wait(mu):
        whole = links.at[mu]
        pltpu.make_async_copy(whole, whole, load_sem.at[mu]).wait()

    def spread_fields(ct):
        row = row_of(ct)
        for f, value in enumerate(fields_of(tile_of(links, 1, row))):
            along_y[f, pl.ds(row, 8), :] = value
        wide = wide_row(ct)
        for f, value in enumerate(fields_of(tile_of(links, 2, row))):
            along_z[f, pl.ds(wide + 8, 8), :] = value

    def gather_fields(ct):
        row = row_of(ct)
        wide = wide_row(ct)
        previous = pl.multiple_of(((ct + 7) % 8) * 8, 8)
        column = pl.multiple_of(ct * 128, 128)
        in_x = fields_of(tile_of(links, 0, row))
        for f in range(8):
            total = before_x(in_x[f]) - in_x[f]
            here = along_y[f, pl.ds(row, 8), :]
            total += pltpu.roll(jnp.where(low_96, here, along_y[f, pl.ds(previous, 8), :]), 32, 1) - here
            total += along_z[f, pl.ds(wide + 7, 8), :] - along_z[f, pl.ds(wide + 8, 8), :]
            delta[pl.ds(f * 8, 8), pl.ds(column, 128)] = total
        for f, value in enumerate(fields_of(tile_of(links, 3, row))):
            delta[pl.ds(64 + f * 8, 8), pl.ds(column, 128)] = value

    def each_tile(body):
        def step(ct, carry):
            body(ct)
            return carry

        lax.fori_loop(0, 8, step, 0)

    def exchange_start(slot):
        source = exchange.at[slot]
        place = exchange.at[slot + 1]
        mine = pl.ds(pl.multiple_of(me * 8, 8), 8)
        pltpu.make_async_copy(source.at[mine], place.at[mine], recv_sem.at[slot // 2]).start()
        for offset in OFFSETS:
            to_ta, to_gz = target(offset)
            chunk = pl.ds(pl.multiple_of((to_ta * NGZ + to_gz) * 8, 8), 8)
            pltpu.make_async_remote_copy(
                source.at[chunk],
                place.at[mine],
                send_sem.at[slot // 2],
                recv_sem.at[slot // 2],
                device_id={"ta": to_ta, "gz": to_gz},
                device_id_type=MESH,
            ).start()

    def exchange_wait(slot):
        whole = exchange.at[slot + 1]
        pltpu.make_async_copy(whole, whole, recv_sem.at[slot // 2]).wait()

    def exchange_sent(slot):
        part = exchange.at[slot, pl.ds(0, 1016)]
        pltpu.make_async_copy(part, part, send_sem.at[slot // 2]).wait()

    def product_nt(left_hi, left_lo, right):
        high, low = split(right)
        both = jnp.concatenate([high, low], axis=0)
        dims = (((1,), (1,)), ((), ()))
        wide = lax.dot_general(left_hi, both, dims, preferred_element_type=F32)
        return wide[:, 0:128] + wide[:, 128:256] + lax.dot_general(left_lo, high, dims, preferred_element_type=F32)

    def plane_forward(slot):
        x0, x1, x2, x3 = [delta[:, a * 256 : (a + 1) * 256] for a in range(4)]
        p, m, q, n = x0 + x2, x0 - x2, x1 + x3, x1 - x3
        exchange[slot, 0:256, :] = product_nt(even_hi[0:256, :], even_lo[0:256, :], p + q)
        exchange[slot, 256:512, :] = product_nt(even_hi[256:512, :], even_lo[256:512, :], p - q)
        exchange[slot, 512:1024, :] = product_nt(odd_hi[...], odd_lo[...], jnp.concatenate([m, n], axis=1))

    def product_tn(left, right_hi, right_lo):
        turned_left = jnp.concatenate(
            [left[i * 128 : (i + 1) * 128, :].T for i in range(left.shape[0] // 128)], axis=1
        )
        high, low = split(turned_left)
        tall = jnp.dot(jnp.concatenate([high, low], axis=0), right_hi, preferred_element_type=F32)
        return tall[0:128] + tall[128:256] + jnp.dot(high, right_lo, preferred_element_type=F32)

    def plane_backward(slot):
        b0 = product_tn(exchange[slot, 0:256, :], even_hi[0:256, :], even_lo[0:256, :])
        b2 = product_tn(exchange[slot, 256:512, :], even_hi[256:512, :], even_lo[256:512, :])
        odd = product_tn(exchange[slot, 512:1024, :], odd_hi[...], odd_lo[...])
        c, s = odd[:, 0:256], odd[:, 256:512]
        plus, minus = b0 + b2, b0 - b2
        for a, value in enumerate((plus + c, minus + s, plus - c, minus - s)):
            for side in range(2):
                ct = 2 * a + side
                for sf in range(16):
                    smooth[sf, ct * 8 : ct * 8 + 8, :] = value[sf * 8 : sf * 8 + 8, side * 128 : side * 128 + 128]

    tall_lane = lax.broadcasted_iota(jnp.int32, (128, 128), 1)
    in_space = tall_lane < 64

    def line_filter(slot):
        parts = []
        for j in range(8):
            got = exchange[slot, pl.ds(j, 128, stride=8), :]
            late = jnp.concatenate([got[120:128], got[0:120]], axis=0)
            parts.append(jnp.where(in_space, got, late - got))
        high, low = split(jnp.concatenate(parts, axis=1))
        stacked = jnp.concatenate([high, low], axis=0)
        lines = jnp.dot(firsts[0], stacked, preferred_element_type=F32)
        lines += jnp.dot(firsts[1, :, 0:128], high, preferred_element_type=F32)
        back = [[None] * 8 for _ in range(8)]
        for p in range(4):
            rows = []
            for j in range(8):
                rows.append(
                    jnp.concatenate(
                        [lines[p * 32 + h * 16 : p * 32 + h * 16 + 16, j * 128 : j * 128 + 128] for h in range(2)],
                        axis=1,
                    )
                )
            high, low = split(jnp.concatenate(rows, axis=0))
            wide = jnp.dot(high, seconds[p], preferred_element_type=F32)
            modes = wide[:, 0:128] + wide[:, 128:256]
            modes += jnp.dot(low, seconds[p, :, 0:128], preferred_element_type=F32)
            modes = modes * weight[p]
            high, low = split(modes)
            turn_hi = turned[p, 0:128, :]
            near = jnp.dot(high, turn_hi, preferred_element_type=F32)
            near += jnp.dot(low, turn_hi, preferred_element_type=F32)
            near += jnp.dot(high, turned[p, 128:256, :], preferred_element_type=F32)
            for j in range(8):
                for h in range(2):
                    back[2 * p + h][j] = near[j * 16 : j * 16 + 16, h * 128 : h * 128 + 128]
        high, low = split(jnp.concatenate([jnp.concatenate(row, axis=1) for row in back], axis=0))
        stacked = jnp.concatenate([high, low], axis=0)
        sites = jnp.dot(firsts[2], stacked, preferred_element_type=F32)
        sites += jnp.dot(firsts[3, :, 0:128], high, preferred_element_type=F32)
        for j in range(8):
            here = sites[:, j * 128 : j * 128 + 128]
            early = jnp.concatenate([here[8:128], here[0:8]], axis=0)
            exchange[slot + 1, pl.ds(j, 128, stride=8), :] = jnp.where(in_space, here, early)

    def store_gauge(ref, row, matrix):
        for i in range(3):
            for k in range(3):
                for part in range(2):
                    ref[part, i, k, pl.ds(row, 8), :] = matrix[i][k][part]

    def load_gauge(ref, window):
        return [[(ref[0, i, k, window, :], ref[1, i, k, window, :]) for k in range(3)] for i in range(3)]

    def make_gauge(ct):
        row = row_of(ct)
        store_gauge(gauge, wide_row(ct), gauge_of([smooth[f, pl.ds(row, 8), :] for f in range(8)]))
        store_gauge(ahead, row, gauge_of([smooth[8 + f, pl.ds(row, 8), :] for f in range(8)]))

    def store_link(mu, row, rows):
        for i in range(3):
            for k in range(3):
                for part in range(2):
                    links[mu, part, i, k, pl.ds(row, 8), :] = rows[i][k][part]

    def mapped(left, fn):
        return [[(fn(re), fn(im)) for re, im in row] for row in left]

    def rotate_xyt(ct):
        row = row_of(ct)
        left = load_gauge(gauge, pl.ds(wide_row(ct), 8))
        store_link(0, row, rotated_link(left, tile_of(links, 0, row), mapped(left, after_x)))
        following = load_gauge(gauge, pl.ds(pl.multiple_of(((ct + 1) % 8) * 16, 16), 8))
        right = [
            [
                tuple(pltpu.roll(jnp.where(low_32, following[i][k][part], left[i][k][part]), 96, 1) for part in range(2))
                for k in range(3)
            ]
            for i in range(3)
        ]
        store_link(1, row, rotated_link(left, tile_of(links, 1, row), right))
        store_link(3, row, rotated_link(left, tile_of(links, 3, row), load_gauge(ahead, pl.ds(row, 8))))

    def rotate_z(ct):
        row = row_of(ct)
        wide = wide_row(ct)
        left = load_gauge(gauge, pl.ds(wide, 8))
        right = load_gauge(gauge, pl.ds(wide + 1, 8))
        store_link(2, row, rotated_link(left, tile_of(links, 2, row), right))

    def edge_copy(way, device):
        return pltpu.make_async_remote_copy(
            edge_out.at[way], edge_in.at[way], edge_send_sem.at[way], edge_recv_sem.at[way], device_id=device,
            device_id_type=MESH,
        )

    load_wait(1)
    load_wait(2)
    for part in range(2):
        for i in range(3):
            for k in range(3):
                link_out[part, i, k] = links[2, part, i, k, pl.ds(7, 8, stride=8), :]
    each_tile(spread_fields)
    load_wait(0)
    load_wait(3)
    tables[7].wait()
    tables[8].wait()
    scale = 16.0 * 0.02 / (LX * LY * LZ * LT)
    for p in range(4):
        for j in range(8):
            total = weight[p, j * 16 : j * 16 + 16, :] + sine[j : j + 1, :]
            empty = total < 1e-6
            weight[p, j * 16 : j * 16 + 16, :] = jnp.where(empty, 0.0, scale / jnp.where(empty, 1.0, total))
    for index in range(7):
        tables[index].wait()
    pl.semaphore_wait(barrier, DEVICES - 1)
    link_copy = pltpu.make_async_remote_copy(
        link_out, link_in, edge_send_sem.at[4], edge_recv_sem.at[4], device_id=after, device_id_type=MESH
    )
    link_copy.start()
    link_copy.wait_recv()
    for f, value in enumerate(fields_of(lambda part, i, k: link_in[part, i, k])):
        along_z[f, pl.ds(7, 8, stride=16), :] = value

    for iteration in range(ITERS):
        last = iteration + 1 == ITERS
        slot = 4 * iteration
        each_tile(gather_fields)
        plane_forward(slot)
        exchange_start(slot)
        exchange_wait(slot)
        line_filter(slot + 1)
        exchange_start(slot + 2)
        exchange_wait(slot + 2)
        plane_backward(slot + 3)
        high_way, low_way = 2 * iteration, 2 * iteration + 1
        for f in range(8):
            edge_out[high_way, f] = smooth[f, pl.ds(0, 8, stride=8), :]
        to_before = edge_copy(high_way, before)
        to_before.start()
        if not last:
            for f in range(8):
                edge_out[low_way, f] = smooth[f, pl.ds(7, 8, stride=8), :]
            to_after = edge_copy(low_way, after)
            to_after.start()
        each_tile(make_gauge)
        each_tile(rotate_xyt)
        if last:
            for mu in (0, 1, 3):
                for ct in range(8):
                    pltpu.make_async_copy(
                        links.at[mu, :, :, :, pl.ds(ct * 8, 8), :],
                        out_hbm.at[mu, :, :, :, 0, :, pl.ds(ct * 128, 128)],
                        store_sem.at[mu],
                    ).start()
        to_before.wait_recv()
        halo = gauge_of([edge_in[high_way, f] for f in range(8)])
        for part in range(2):
            for i in range(3):
                for k in range(3):
                    gauge[part, i, k, pl.ds(8, 8, stride=16), :] = halo[i][k][part]
        each_tile(rotate_z)
        if last:
            for ct in range(8):
                pltpu.make_async_copy(
                    links.at[2, :, :, :, pl.ds(ct * 8, 8), :],
                    out_hbm.at[2, :, :, :, 0, :, pl.ds(ct * 128, 128)],
                    store_sem.at[2],
                ).start()
        else:
            to_after.wait_recv()
            left = gauge_of([edge_in[low_way, f] for f in range(8)])
            right = load_gauge(gauge, pl.ds(0, 8, stride=16))
            below = rotated_link(left, lambda part, i, k: link_in[part, i, k], right)
            each_tile(spread_fields)
            for f, value in enumerate(fields_of(lambda part, i, k: below[i][k][part])):
                along_z[f, pl.ds(7, 8, stride=16), :] = value
            to_after.wait_send()
        to_before.wait_send()

    link_copy.wait_send()
    for slot in range(0, 4 * ITERS, 2):
        exchange_sent(slot)
    for mu in range(4):
        whole = links.at[mu]
        pltpu.make_async_copy(whole, whole, store_sem.at[mu]).wait()


def on_device(gauge_links):
    tables = make_tables()
    operands = [jnp.asarray(table) for table in tables]
    anywhere = pl.BlockSpec(memory_space=pl.ANY)
    scratch = [
        pltpu.VMEM((4, 2, 3, 3, 64, 128), F32),
        pltpu.VMEM((512, 256), BF16),
        pltpu.VMEM((512, 256), BF16),
        pltpu.VMEM((512, 512), BF16),
        pltpu.VMEM((512, 512), BF16),
        pltpu.VMEM((4, 128, 256), BF16),
        pltpu.VMEM((4, 256, 256), BF16),
        pltpu.VMEM((4, 256, 256), BF16),
        pltpu.VMEM((4, 128, 128), F32),
        pltpu.VMEM((8, 128), F32),
        pltpu.VMEM((128, 1024), F32),
        pltpu.VMEM((8, 64, 128), F32),
        pltpu.VMEM((8, 128, 128), F32),
        pltpu.VMEM((4 * ITERS, 1024, 128), F32),
        pltpu.VMEM((16, 64, 128), F32),
        pltpu.VMEM((2, 3, 3, 128, 128), F32),
        pltpu.VMEM((2, 3, 3, 64, 128), F32),
        pltpu.VMEM((2, 3, 3, 8, 128), F32),
        pltpu.VMEM((2, 3, 3, 8, 128), F32),
        pltpu.VMEM((4, 8, 8, 128), F32),
        pltpu.VMEM((4, 8, 8, 128), F32),
        pltpu.SemaphoreType.DMA((9,)),
        pltpu.SemaphoreType.DMA((4,)),
        pltpu.SemaphoreType.DMA((4,)),
        pltpu.SemaphoreType.DMA((2 * ITERS,)),
        pltpu.SemaphoreType.DMA((2 * ITERS,)),
        pltpu.SemaphoreType.DMA((5,)),
        pltpu.SemaphoreType.DMA((5,)),
    ]
    return pl.pallas_call(
        kernel,
        out_shape=jax.ShapeDtypeStruct(gauge_links.shape, F32),
        in_specs=[anywhere] * (1 + len(operands)),
        out_specs=anywhere,
        scratch_shapes=scratch,
        compiler_params=pltpu.CompilerParams(
            collective_id=0, has_side_effects=True, vmem_limit_bytes=48 * 1024 * 1024
        ),
    )(gauge_links, *operands)


def solution(mesh):
    specs = P(None, None, None, None, "ta", "gz", None)
    return jax.shard_map(on_device, mesh=mesh, in_specs=(specs,), out_specs=specs, check_vma=False)
```

```python
import functools

import jax
import jax.numpy as jnp
import ml_dtypes
import numpy as np
from jax import lax
from jax.experimental import pallas as pl
from jax.experimental.pallas import tpu as pltpu
from jax.sharding import PartitionSpec as P

LX = 32
LY = 32
LZ = 64
LT = 16
ITERS = 2
NTA = 16
NGZ = 8
DEVICES = NTA * NGZ
SPARE_ROWS = 16384
MESH = pl.DeviceIdType.MESH
F32 = jnp.float32
BF16 = jnp.bfloat16


def cas(angle):
    return np.cos(angle) + np.sin(angle)


def halves(table):
    high = table.astype(ml_dtypes.bfloat16)
    low = (table - high.astype(np.float64)).astype(ml_dtypes.bfloat16)
    return high, low


def plane_modes():
    wave_y = [k for k in range(LY) if k % 4 == 0]
    wave_y += [k for k in range(LY) if k % 4 == 2]
    wave_y += [k for k in range(LY) if k % 2 == 1]
    return np.repeat(np.array(wave_y), LX), np.tile(np.arange(LX), LY)


def plane_tables():
    ky, kx = plane_modes()
    b = np.repeat(np.arange(8), LX)
    x = np.tile(np.arange(LX), 8)
    along_x = cas(2 * np.pi * (kx[:, None] * x[None, :] % LX) / LX)
    phase = 2 * np.pi * (ky[:, None] * b[None, :] % LY) / LY
    plain = cas(phase) * along_x
    sign = np.where(ky % 4 == 1, 1.0, -1.0)[:, None]
    mirrored = sign * cas(-phase) * along_x
    even = plain[0:512]
    odd = np.concatenate([plain[512:], mirrored[512:]], axis=1)
    return halves(even) + halves(odd)


def line_tables():
    t = np.arange(LT)
    along_t = cas(2 * np.pi * (t[:, None] * t[None, :] % LT) / LT)
    zb = np.arange(8)
    waves = [np.cos(0 * zb), np.cos(np.pi * zb)]
    for k in (1, 2, 3):
        waves += [np.cos(2 * np.pi * k * zb / 8), np.sin(2 * np.pi * k * zb / 8)]
    waves = np.stack(waves)
    first = np.einsum("qz,kt->qktz", waves, along_t).reshape(128, 128)
    z8 = np.arange(8)
    second = np.zeros((4, 2, 2, 8, 8, 8, 16))
    depth = np.zeros((4, 16), np.int64)
    for pair in range(4):
        for j in range(16):
            k1 = (0, 4)[j // 8] if pair == 0 else (pair, 8 - pair)[j // 8]
            kz = k1 + 8 * (j % 8)
            depth[pair, j] = kz
            beta = 2 * np.pi * (kz * z8 % LZ) / LZ
            for f in range(8):
                for s in range(2):
                    if pair == 0:
                        second[pair, j // 8, s, f, :, f, j] = cas(beta)
                    else:
                        second[pair, 0, s, f, :, f, j] = cas(beta)
                        second[pair, 1, s, f, :, f, j] = (1.0 if j < 8 else -1.0) * cas(-beta)
    second = second.reshape(4, 256, 128)
    sine_t = 4 * np.sin(np.pi * t / LT) ** 2
    sine_z = 4 * np.sin(np.pi * depth / LZ) ** 2
    base = np.zeros((4, 8, 16, 8, 16))
    base += sine_t[None, None, :, None, None] + sine_z[:, None, None, None, :]
    return first, second, base.reshape(4, 128, 128).astype(np.float32)


def make_tables():
    plane = plane_tables()
    first, second, base = line_tables()
    first_hi, first_lo = halves(first)
    back_hi, back_lo = halves(first.T)
    second_hi, second_lo = halves(second)
    turned_hi, turned_lo = halves(np.swapaxes(second, 1, 2))
    firsts = np.stack(
        [
            np.concatenate([first_hi, first_hi], axis=1),
            np.concatenate([first_lo, np.zeros_like(first_lo)], axis=1),
            np.concatenate([back_hi, back_hi], axis=1),
            np.concatenate([back_lo, np.zeros_like(back_lo)], axis=1),
        ]
    )
    seconds = np.concatenate([second_hi, second_lo], axis=2)
    turned = np.concatenate([turned_hi, turned_lo], axis=1)
    blocks = [plane[0], plane[1]]
    for part in (plane[2], plane[3]):
        blocks += [part[:, 0:256], part[:, 256:512]]
    blocks += [firsts.reshape(512, 256), seconds.reshape(1024, 256), turned.reshape(1024, 256)]
    ky, kx = plane_modes()
    sine_xy = 4 * np.sin(np.pi * ky / LY) ** 2 + 4 * np.sin(np.pi * kx / LX) ** 2
    sine_xy = np.repeat(sine_xy[:, None], 128, axis=1).astype(np.float32)
    tables = np.concatenate(blocks)
    waves = np.concatenate([base.reshape(512, 128), sine_xy])
    return np.resize(tables, (SPARE_ROWS, 256)), np.resize(waves, (SPARE_ROWS, 128))


def split(value):
    high = value.astype(BF16)
    return high, (value - high.astype(F32)).astype(BF16)


def fields_of(link):
    imag_sum = link(1, 0, 0) + link(1, 1, 1) + link(1, 2, 2)
    third = imag_sum * (2.0 / 3.0)
    return [
        link(0, 0, 1) - link(0, 1, 0),
        link(1, 0, 1) + link(1, 1, 0),
        link(0, 0, 2) - link(0, 2, 0),
        link(1, 0, 2) + link(1, 2, 0),
        link(0, 1, 2) - link(0, 2, 1),
        link(1, 1, 2) + link(1, 2, 1),
        2.0 * link(1, 0, 0) - third,
        2.0 * link(1, 1, 1) - third,
    ]


def inverse_root(value):
    guess = lax.rsqrt(value)
    return guess * (1.5 - 0.5 * value * guess * guess)


def cross_row(first, second):
    out = []
    for position in range(3):
        follow, beyond = (position + 1) % 3, (position + 2) % 3
        fr, fi = first[follow]
        gr, gi = first[beyond]
        sr, si = second[beyond]
        tr, ti = second[follow]
        real = fr * sr - fi * si - (gr * tr - gi * ti)
        imag = gr * ti + gi * tr - (fr * si + fi * sr)
        out.append((real, imag))
    return out


def gauge_of(x):
    a, b, c, d, e, f, d0, d1 = x
    n01 = a * a + b * b
    n02 = c * c + d * d
    n12 = e * e + f * f
    both = d0 + d1
    s01r = -both * b - (c * e + d * f)
    s01i = both * a - (d * e - c * f)
    s02r = d1 * d + (a * e - b * f)
    s02i = (a * f + b * e) - d1 * c
    s12r = d0 * f - (a * c + b * d)
    s12i = (b * c - a * d) - d0 * e
    r0 = [(1.0 - 0.5 * (d0 * d0 + n01 + n02), d0), (a + 0.5 * s01r, b + 0.5 * s01i), (c + 0.5 * s02r, d + 0.5 * s02i)]
    r1 = [(0.5 * s01r - a, b - 0.5 * s01i), (1.0 - 0.5 * (d1 * d1 + n01 + n12), d1), (e + 0.5 * s12r, f + 0.5 * s12i)]

    def unit(row):
        total = None
        for real, imag in row:
            term = real * real + imag * imag
            total = term if total is None else total + term
        scale = inverse_root(total)
        return [(real * scale, imag * scale) for real, imag in row]

    u0 = unit(r0)
    pr = pi = None
    for (ur, ui), (vr, vi) in zip(u0, r1):
        tr, ti = ur * vr + ui * vi, ur * vi - ui * vr
        pr = tr if pr is None else pr + tr
        pi = ti if pi is None else pi + ti
    v = [(vr - (pr * ur - pi * ui), vi - (pr * ui + pi * ur)) for (ur, ui), (vr, vi) in zip(u0, r1)]
    u1 = unit(v)
    return [u0, u1, cross_row(u0, u1)]


def rotated_link(left, link, right):
    rows = []
    for i in range(2):
        product = []
        for k in range(3):
            real = imag = None
            for m in range(3):
                lr, li = left[i][m]
                ur, ui = link(0, m, k), link(1, m, k)
                tr, ti = lr * ur - li * ui, lr * ui + li * ur
                real = tr if real is None else real + tr
                imag = ti if imag is None else imag + ti
            product.append((real, imag))
        row = []
        for j in range(3):
            real = imag = None
            for k in range(3):
                pr, pi = product[k]
                gr, gi = right[j][k]
                tr, ti = pr * gr + pi * gi, pi * gr - pr * gi
                real = tr if real is None else real + tr
                imag = ti if imag is None else imag + ti
            row.append((real, imag))
        rows.append(row)
    rows.append(cross_row(rows[0], rows[1]))
    return rows


def hop_count(offset):
    return sum(min(v, 4 - v) for v in offset[:3]) + 0.1 * offset[3]


OFFSETS = sorted(
    [
        (dx, dy, dz, dc)
        for dy in range(4)
        for dz in range(4)
        for dx in range(4)
        for dc in range(2)
        if dx + dy + dz + dc > 0
    ],
    key=lambda o: -hop_count(o),
)


def target(offset):
    ta = lax.axis_index("ta")
    gz = lax.axis_index("gz")
    y = (2 * (ta // 8) + gz % 2 + offset[1]) % 4
    to_ta = (y // 2) * 8 + (((ta // 2) % 4 + offset[0]) % 4) * 2 + (ta % 2 + offset[3]) % 2
    to_gz = ((gz // 2 + offset[2]) % 4) * 2 + y % 2
    return to_ta, to_gz


def kernel(
    links_hbm,
    tables_hbm,
    waves_hbm,
    out_hbm,
    links,
    tables,
    weight,
    sine,
    delta,
    along_y,
    along_z,
    exchange,
    smooth,
    gauge,
    ahead,
    link_out,
    link_in,
    edge_out,
    edge_in,
    edge,
    edge_modes,
    row_out,
    row_in,
    row_sem,
    table_sem,
    load_sem,
    store_sem,
    send_sem,
    recv_sem,
    edge_send_sem,
    edge_recv_sem,
):
    ta = lax.axis_index("ta")
    gz = lax.axis_index("gz")
    me = ta * NGZ + gz
    after = {"gz": (gz + 1) % NGZ}
    before = {"gz": (gz + NGZ - 1) % NGZ}

    barrier = pltpu.get_barrier_semaphore()
    loads = []
    for mu in (1, 0, 3, 2):
        for ct in range(8):
            copy = pltpu.make_async_copy(
                links_hbm.at[mu, :, :, :, 0, :, pl.ds(ct * 128, 128)],
                links.at[mu, :, :, :, pl.ds(ct * 8, 8), :],
                load_sem.at[mu],
            )
            copy.start()
    table_copies = [
        pltpu.make_async_copy(waves_hbm.at[pl.ds(0, 512)], weight, table_sem.at[0]),
        pltpu.make_async_copy(waves_hbm.at[pl.ds(pl.multiple_of(512 + me * 8, 8), 8)], sine, table_sem.at[1]),
        pltpu.make_async_copy(tables_hbm.at[pl.ds(0, 5632)], tables, table_sem.at[2]),
    ]
    for copy in table_copies:
        copy.start()
    for offset in OFFSETS:
        to_ta, to_gz = target(offset)
        pl.semaphore_signal(barrier, inc=1, device_id={"ta": to_ta, "gz": to_gz}, device_id_type=MESH)

    lane = lax.broadcasted_iota(jnp.int32, (8, 128), 1)
    first_x = lane % LX == 0
    last_x = lane % LX == LX - 1
    low_96 = lane < 96
    low_32 = lane < 32

    def tile_of(ref, mu, row):
        def link(part, i, k):
            return ref[mu, part, i, k, pl.ds(row, 8), :]

        return link

    def before_x(tile):
        return jnp.where(first_x, pltpu.roll(tile, 97, 1), pltpu.roll(tile, 1, 1))

    def after_x(tile):
        return jnp.where(last_x, pltpu.roll(tile, 31, 1), pltpu.roll(tile, 127, 1))

    def row_of(ct):
        return pl.multiple_of(ct * 8, 8)

    def wide_row(ct):
        return pl.multiple_of(ct * 16, 16)

    def load_wait(mu):
        whole = links.at[mu]
        pltpu.make_async_copy(whole, whole, load_sem.at[mu]).wait()

    def spread_fields(ct):
        row = row_of(ct)
        for f, value in enumerate(fields_of(tile_of(links, 1, row))):
            along_y[f, pl.ds(row, 8), :] = value
        wide = wide_row(ct)
        for f, value in enumerate(fields_of(tile_of(links, 2, row))):
            along_z[f, pl.ds(wide + 8, 8), :] = value

    top_row = lax.broadcasted_iota(jnp.int32, (8, 128), 0) == 0

    def edge_fields(ct):
        wide = wide_row(ct)
        column = pl.ds(pl.multiple_of(ct * 128, 128), 128)
        for f in range(8):
            tile = along_z[f, pl.ds(wide + 8, 8), :]
            edge[pl.ds(f * 8, 8), column] = jnp.where(top_row, pltpu.roll(tile, 1, 0), 0.0)
            edge[pl.ds(64 + f * 8, 8), column] = jnp.zeros((8, 128), F32)

    def gather_fields(ct):
        row = row_of(ct)
        wide = wide_row(ct)
        previous = pl.multiple_of(((ct + 7) % 8) * 8, 8)
        column = pl.multiple_of(ct * 128, 128)
        in_x = fields_of(tile_of(links, 0, row))
        for f in range(8):
            total = before_x(in_x[f]) - in_x[f]
            here = along_y[f, pl.ds(row, 8), :]
            total += pltpu.roll(jnp.where(low_96, here, along_y[f, pl.ds(previous, 8), :]), 32, 1) - here
            total += along_z[f, pl.ds(wide + 7, 8), :] - along_z[f, pl.ds(wide + 8, 8), :]
            delta[pl.ds(f * 8, 8), pl.ds(column, 128)] = total
        for f, value in enumerate(fields_of(tile_of(links, 3, row))):
            delta[pl.ds(64 + f * 8, 8), pl.ds(column, 128)] = value

    def each_tile(body):
        def step(ct, carry):
            body(ct)
            return carry

        lax.fori_loop(0, 8, step, 0)

    def exchange_start(slot, with_rows=False):
        source = exchange.at[slot]
        place = exchange.at[slot + 1]
        mine = pl.ds(pl.multiple_of(me * 8, 8), 8)
        pltpu.make_async_copy(source.at[mine], place.at[mine], recv_sem.at[slot // 2]).start()
        for offset in OFFSETS:
            to_ta, to_gz = target(offset)
            chunk = pl.ds(pl.multiple_of((to_ta * NGZ + to_gz) * 8, 8), 8)
            pltpu.make_async_remote_copy(
                source.at[chunk],
                place.at[mine],
                send_sem.at[slot // 2],
                recv_sem.at[slot // 2],
                device_id={"ta": to_ta, "gz": to_gz},
                device_id_type=MESH,
            ).start()
            if with_rows:
                pltpu.make_async_remote_copy(
                    row_out.at[to_ta * NGZ + to_gz],
                    row_in.at[me],
                    row_sem.at[0],
                    row_sem.at[1],
                    device_id={"ta": to_ta, "gz": to_gz},
                    device_id_type=MESH,
                ).start()
        if with_rows:
            pltpu.make_async_copy(row_out.at[me], row_in.at[me], row_sem.at[1]).start()

    def exchange_wait(slot):
        whole = exchange.at[slot + 1]
        pltpu.make_async_copy(whole, whole, recv_sem.at[slot // 2]).wait()

    def exchange_sent(slot):
        part = exchange.at[slot, pl.ds(0, 1016)]
        pltpu.make_async_copy(part, part, send_sem.at[slot // 2]).wait()

    def table(first, count, columns=256):
        return tables[first : first + count, 0:columns]

    def odd_table(part):
        first = 1024 + 1024 * part
        return jnp.concatenate([table(first, 512), table(first + 512, 512)], axis=1)

    def product_nt(left_hi, left_lo, right):
        high, low = split(right)
        both = jnp.concatenate([high, low], axis=0)
        dims = (((1,), (1,)), ((), ()))
        wide = lax.dot_general(left_hi, both, dims, preferred_element_type=F32)
        return wide[:, 0:128] + wide[:, 128:256] + lax.dot_general(left_lo, high, dims, preferred_element_type=F32)

    def plane_forward(source, place):
        x0, x1, x2, x3 = [source[:, a * 256 : (a + 1) * 256] for a in range(4)]
        p, m, q, n = x0 + x2, x0 - x2, x1 + x3, x1 - x3
        place[0:256, :] = product_nt(table(0, 256), table(512, 256), p + q)
        place[256:512, :] = product_nt(table(256, 256), table(768, 256), p - q)
        place[512:1024, :] = product_nt(odd_table(0), odd_table(1), jnp.concatenate([m, n], axis=1))

    def product_tn(left, right_hi, right_lo):
        turned_left = jnp.concatenate(
            [left[i * 128 : (i + 1) * 128, :].T for i in range(left.shape[0] // 128)], axis=1
        )
        high, low = split(turned_left)
        tall = jnp.dot(jnp.concatenate([high, low], axis=0), right_hi, preferred_element_type=F32)
        return tall[0:128] + tall[128:256] + jnp.dot(high, right_lo, preferred_element_type=F32)

    def plane_backward(slot):
        b0 = product_tn(exchange[slot, 0:256, :], table(0, 256), table(512, 256))
        b2 = product_tn(exchange[slot, 256:512, :], table(256, 256), table(768, 256))
        odd = product_tn(exchange[slot, 512:1024, :], odd_table(0), odd_table(1))
        c, s = odd[:, 0:256], odd[:, 256:512]
        plus, minus = b0 + b2, b0 - b2
        for a, value in enumerate((plus + c, minus + s, plus - c, minus - s)):
            for side in range(2):
                ct = 2 * a + side
                for sf in range(16):
                    smooth[sf, ct * 8 : ct * 8 + 8, :] = value[sf * 8 : sf * 8 + 8, side * 128 : side * 128 + 128]

    tall_lane = lax.broadcasted_iota(jnp.int32, (128, 128), 1)
    in_space = tall_lane < 64

    row_start = in_space & (tall_lane % 8 == 0)

    def pack_rows():
        total = edge_modes[pl.ds(0, 128, stride=8), :]
        for j in range(1, 8):
            total += pltpu.roll(edge_modes[pl.ds(j, 128, stride=8), :], j, 1)
        row_out[...] = total.reshape(128, 1, 128)

    def line_filter(slot, with_rows=False):
        parts = []
        if with_rows:
            rows = row_in[...].reshape(16, 8, 128)
            rows = pltpu.roll(rows, 1, 1).reshape(128, 128)
        for j in range(8):
            got = exchange[slot, pl.ds(j, 128, stride=8), :]
            late = jnp.concatenate([got[120:128], got[0:120]], axis=0)
            part = jnp.where(in_space, got, late - got)
            if with_rows:
                part += jnp.where(row_start, pltpu.roll(rows, 128 - j, 1) if j else rows, 0.0)
            parts.append(part)
        high, low = split(jnp.concatenate(parts, axis=1))
        stacked = jnp.concatenate([high, low], axis=0)
        lines = jnp.dot(table(3072, 128), stacked, preferred_element_type=F32)
        lines += jnp.dot(table(3200, 128, 128), high, preferred_element_type=F32)
        back = [[None] * 8 for _ in range(8)]
        for p in range(4):
            rows = []
            for j in range(8):
                rows.append(
                    jnp.concatenate(
                        [lines[p * 32 + h * 16 : p * 32 + h * 16 + 16, j * 128 : j * 128 + 128] for h in range(2)],
                        axis=1,
                    )
                )
            high, low = split(jnp.concatenate(rows, axis=0))
            wide = jnp.dot(high, table(3584 + 256 * p, 256), preferred_element_type=F32)
            modes = wide[:, 0:128] + wide[:, 128:256]
            modes += jnp.dot(low, table(3584 + 256 * p, 256, 128), preferred_element_type=F32)
            modes = modes * weight[p * 128 : p * 128 + 128, :]
            high, low = split(modes)
            turn_hi = table(4608 + 256 * p, 128)
            near = jnp.dot(high, turn_hi, preferred_element_type=F32)
            near += jnp.dot(low, turn_hi, preferred_element_type=F32)
            near += jnp.dot(high, table(4736 + 256 * p, 128), preferred_element_type=F32)
            for j in range(8):
                for h in range(2):
                    back[2 * p + h][j] = near[j * 16 : j * 16 + 16, h * 128 : h * 128 + 128]
        high, low = split(jnp.concatenate([jnp.concatenate(row, axis=1) for row in back], axis=0))
        stacked = jnp.concatenate([high, low], axis=0)
        sites = jnp.dot(table(3328, 128), stacked, preferred_element_type=F32)
        sites += jnp.dot(table(3456, 128, 128), high, preferred_element_type=F32)
        for j in range(8):
            here = sites[:, j * 128 : j * 128 + 128]
            early = jnp.concatenate([here[8:128], here[0:8]], axis=0)
            exchange[slot + 1, pl.ds(j, 128, stride=8), :] = jnp.where(in_space, here, early)

    def store_gauge(ref, row, matrix):
        for i in range(3):
            for k in range(3):
                for part in range(2):
                    ref[part, i, k, pl.ds(row, 8), :] = matrix[i][k][part]

    def load_gauge(ref, window):
        return [[(ref[0, i, k, window, :], ref[1, i, k, window, :]) for k in range(3)] for i in range(3)]

    def make_gauge(ct):
        row = row_of(ct)
        store_gauge(gauge, wide_row(ct), gauge_of([smooth[f, pl.ds(row, 8), :] for f in range(8)]))
        store_gauge(ahead, row, gauge_of([smooth[8 + f, pl.ds(row, 8), :] for f in range(8)]))

    def store_link(mu, row, rows):
        for i in range(3):
            for k in range(3):
                for part in range(2):
                    links[mu, part, i, k, pl.ds(row, 8), :] = rows[i][k][part]

    def mapped(left, fn):
        return [[(fn(re), fn(im)) for re, im in row] for row in left]

    def rotate_xyt(ct):
        row = row_of(ct)
        left = load_gauge(gauge, pl.ds(wide_row(ct), 8))
        store_link(0, row, rotated_link(left, tile_of(links, 0, row), mapped(left, after_x)))
        following = load_gauge(gauge, pl.ds(pl.multiple_of(((ct + 1) % 8) * 16, 16), 8))
        right = [
            [
                tuple(pltpu.roll(jnp.where(low_32, following[i][k][part], left[i][k][part]), 96, 1) for part in range(2))
                for k in range(3)
            ]
            for i in range(3)
        ]
        store_link(1, row, rotated_link(left, tile_of(links, 1, row), right))
        store_link(3, row, rotated_link(left, tile_of(links, 3, row), load_gauge(ahead, pl.ds(row, 8))))

    def rotate_z(ct):
        row = row_of(ct)
        wide = wide_row(ct)
        left = load_gauge(gauge, pl.ds(wide, 8))
        right = load_gauge(gauge, pl.ds(wide + 1, 8))
        store_link(2, row, rotated_link(left, tile_of(links, 2, row), right))

    def edge_copy(way, device):
        return pltpu.make_async_remote_copy(
            edge_out.at[way], edge_in.at[way], edge_send_sem.at[way], edge_recv_sem.at[way], device_id=device,
            device_id_type=MESH,
        )

    load_wait(1)
    load_wait(2)
    for part in range(2):
        for i in range(3):
            for k in range(3):
                link_out[part, i, k] = links[2, part, i, k, pl.ds(7, 8, stride=8), :]
    each_tile(spread_fields)
    load_wait(0)
    load_wait(3)
    table_copies[0].wait()
    table_copies[1].wait()
    scale = 16.0 * 0.02 / (LX * LY * LZ * LT)
    for p in range(4):
        for j in range(8):
            total = weight[p * 128 + j * 16 : p * 128 + j * 16 + 16, :] + sine[j : j + 1, :]
            empty = total < 1e-6
            weight[p * 128 + j * 16 : p * 128 + j * 16 + 16, :] = jnp.where(empty, 0.0, scale / jnp.where(empty, 1.0, total))
    table_copies[2].wait()
    for f in range(8):
        along_z[f, pl.ds(7, 8, stride=16), :] = jnp.zeros((8, 128), F32)
    each_tile(gather_fields)
    each_tile(edge_fields)
    plane_forward(edge, edge_modes)
    pack_rows()
    plane_forward(delta, exchange.at[0])
    pl.semaphore_wait(barrier, DEVICES - 1)
    exchange_start(0, True)
    link_copy = pltpu.make_async_remote_copy(
        link_out, link_in, edge_send_sem.at[4], edge_recv_sem.at[4], device_id=after, device_id_type=MESH
    )
    link_copy.start()

    for iteration in range(ITERS):
        last = iteration + 1 == ITERS
        slot = 4 * iteration
        if iteration > 0:
            each_tile(gather_fields)
            plane_forward(delta, exchange.at[slot])
            exchange_start(slot)
        else:
            pltpu.make_async_copy(row_in, row_in, row_sem.at[1]).wait()
        exchange_wait(slot)
        line_filter(slot + 1, iteration == 0)
        exchange_start(slot + 2)
        exchange_wait(slot + 2)
        plane_backward(slot + 3)
        high_way, low_way = 2 * iteration, 2 * iteration + 1
        for f in range(8):
            edge_out[high_way, f] = smooth[f, pl.ds(0, 8, stride=8), :]
        to_before = edge_copy(high_way, before)
        to_before.start()
        if not last:
            for f in range(8):
                edge_out[low_way, f] = smooth[f, pl.ds(7, 8, stride=8), :]
            to_after = edge_copy(low_way, after)
            to_after.start()
        each_tile(make_gauge)
        each_tile(rotate_xyt)
        if last:
            for mu in (0, 1, 3):
                for ct in range(8):
                    pltpu.make_async_copy(
                        links.at[mu, :, :, :, pl.ds(ct * 8, 8), :],
                        out_hbm.at[mu, :, :, :, 0, :, pl.ds(ct * 128, 128)],
                        store_sem.at[mu],
                    ).start()
        to_before.wait_recv()
        halo = gauge_of([edge_in[high_way, f] for f in range(8)])
        for part in range(2):
            for i in range(3):
                for k in range(3):
                    gauge[part, i, k, pl.ds(8, 8, stride=16), :] = halo[i][k][part]
        each_tile(rotate_z)
        if last:
            for ct in range(8):
                pltpu.make_async_copy(
                    links.at[2, :, :, :, pl.ds(ct * 8, 8), :],
                    out_hbm.at[2, :, :, :, 0, :, pl.ds(ct * 128, 128)],
                    store_sem.at[2],
                ).start()
        else:
            to_after.wait_recv()
            link_copy.wait_recv()
            left = gauge_of([edge_in[low_way, f] for f in range(8)])
            right = load_gauge(gauge, pl.ds(0, 8, stride=16))
            below = rotated_link(left, lambda part, i, k: link_in[part, i, k], right)
            each_tile(spread_fields)
            for f, value in enumerate(fields_of(lambda part, i, k: below[i][k][part])):
                along_z[f, pl.ds(7, 8, stride=16), :] = value
            to_after.wait_send()
        to_before.wait_send()

    link_copy.wait_send()
    pltpu.make_async_copy(row_out.at[pl.ds(0, 127)], row_out.at[pl.ds(0, 127)], row_sem.at[0]).wait()
    for slot in range(0, 4 * ITERS, 2):
        exchange_sent(slot)
    for mu in range(4):
        whole = links.at[mu]
        pltpu.make_async_copy(whole, whole, store_sem.at[mu]).wait()


def on_device(gauge_links):
    operands = [jnp.asarray(table) for table in make_tables()]
    anywhere = pl.BlockSpec(memory_space=pl.ANY)
    scratch = [
        pltpu.VMEM((4, 2, 3, 3, 64, 128), F32),
        pltpu.VMEM((5632, 256), BF16),
        pltpu.VMEM((512, 128), F32),
        pltpu.VMEM((8, 128), F32),
        pltpu.VMEM((128, 1024), F32),
        pltpu.VMEM((8, 64, 128), F32),
        pltpu.VMEM((8, 128, 128), F32),
        pltpu.VMEM((4 * ITERS, 1024, 128), F32),
        pltpu.VMEM((16, 64, 128), F32),
        pltpu.VMEM((2, 3, 3, 128, 128), F32),
        pltpu.VMEM((2, 3, 3, 64, 128), F32),
        pltpu.VMEM((2, 3, 3, 8, 128), F32),
        pltpu.VMEM((2, 3, 3, 8, 128), F32),
        pltpu.VMEM((4, 8, 8, 128), F32),
        pltpu.VMEM((4, 8, 8, 128), F32),
        pltpu.VMEM((128, 1024), F32),
        pltpu.VMEM((1024, 128), F32),
        pltpu.VMEM((128, 1, 128), F32),
        pltpu.VMEM((128, 1, 128), F32),
        pltpu.SemaphoreType.DMA((2,)),
        pltpu.SemaphoreType.DMA((3,)),
        pltpu.SemaphoreType.DMA((4,)),
        pltpu.SemaphoreType.DMA((4,)),
        pltpu.SemaphoreType.DMA((2 * ITERS,)),
        pltpu.SemaphoreType.DMA((2 * ITERS,)),
        pltpu.SemaphoreType.DMA((5,)),
        pltpu.SemaphoreType.DMA((5,)),
    ]
    return pl.pallas_call(
        kernel,
        out_shape=jax.ShapeDtypeStruct(gauge_links.shape, F32),
        in_specs=[anywhere] * (1 + len(operands)),
        out_specs=anywhere,
        scratch_shapes=scratch,
        compiler_params=pltpu.CompilerParams(
            collective_id=0, has_side_effects=True, vmem_limit_bytes=50 * 1024 * 1024
        ),
    )(gauge_links, *operands)


def solution(mesh):
    specs = P(None, None, None, None, "ta", "gz", None)
    return jax.shard_map(on_device, mesh=mesh, in_specs=(specs,), out_specs=specs, check_vma=False)
```

```python
import functools

import jax
import jax.numpy as jnp
import ml_dtypes
import numpy as np
from jax import lax
from jax.experimental import pallas as pl
from jax.experimental.pallas import tpu as pltpu
from jax.sharding import PartitionSpec as P

LX = 32
LY = 32
LZ = 64
LT = 16
ITERS = 2
NTA = 16
NGZ = 8
DEVICES = NTA * NGZ
SPARE_ROWS = 16384
MESH = pl.DeviceIdType.MESH
F32 = jnp.float32
BF16 = jnp.bfloat16


def cas(angle):
    return np.cos(angle) + np.sin(angle)


def halves(table):
    high = table.astype(ml_dtypes.bfloat16)
    low = (table - high.astype(np.float64)).astype(ml_dtypes.bfloat16)
    return high, low


def plane_modes():
    wave_y = [k for k in range(LY) if k % 4 == 0]
    wave_y += [k for k in range(LY) if k % 4 == 2]
    wave_y += [k for k in range(LY) if k % 2 == 1]
    return np.repeat(np.array(wave_y), LX), np.tile(np.arange(LX), LY)


def plane_tables():
    ky, kx = plane_modes()
    b = np.repeat(np.arange(8), LX)
    x = np.tile(np.arange(LX), 8)
    along_x = cas(2 * np.pi * (kx[:, None] * x[None, :] % LX) / LX)
    phase = 2 * np.pi * (ky[:, None] * b[None, :] % LY) / LY
    plain = cas(phase) * along_x
    sign = np.where(ky % 4 == 1, 1.0, -1.0)[:, None]
    mirrored = sign * cas(-phase) * along_x
    even = plain[0:512]
    odd = np.concatenate([plain[512:], mirrored[512:]], axis=1)
    return halves(even) + halves(odd)


def line_tables():
    t = np.arange(LT)
    along_t = cas(2 * np.pi * (t[:, None] * t[None, :] % LT) / LT)
    zb = np.arange(8)
    waves = [np.cos(0 * zb), np.cos(np.pi * zb)]
    for k in (1, 2, 3):
        waves += [np.cos(2 * np.pi * k * zb / 8), np.sin(2 * np.pi * k * zb / 8)]
    waves = np.stack(waves)
    first = np.einsum("qz,kt->qktz", waves, along_t).reshape(128, 128)
    z8 = np.arange(8)
    second = np.zeros((4, 2, 2, 8, 8, 8, 16))
    depth = np.zeros((4, 16), np.int64)
    for pair in range(4):
        for j in range(16):
            k1 = (0, 4)[j // 8] if pair == 0 else (pair, 8 - pair)[j // 8]
            kz = k1 + 8 * (j % 8)
            depth[pair, j] = kz
            beta = 2 * np.pi * (kz * z8 % LZ) / LZ
            for f in range(8):
                for s in range(2):
                    if pair == 0:
                        second[pair, j // 8, s, f, :, f, j] = cas(beta)
                    else:
                        second[pair, 0, s, f, :, f, j] = cas(beta)
                        second[pair, 1, s, f, :, f, j] = (1.0 if j < 8 else -1.0) * cas(-beta)
    second = second.reshape(4, 256, 128)
    sine_t = 4 * np.sin(np.pi * t / LT) ** 2
    sine_z = 4 * np.sin(np.pi * depth / LZ) ** 2
    base = np.zeros((4, 8, 16, 8, 16))
    base += sine_t[None, None, :, None, None] + sine_z[:, None, None, None, :]
    return first, second, base.reshape(4, 128, 128).astype(np.float32)


def make_tables():
    plane = plane_tables()
    first, second, base = line_tables()
    first_hi, first_lo = halves(first)
    back_hi, back_lo = halves(first.T)
    second_hi, second_lo = halves(second)
    turned_hi, turned_lo = halves(np.swapaxes(second, 1, 2))
    firsts = np.stack(
        [
            np.concatenate([first_hi, first_hi], axis=1),
            np.concatenate([first_lo, np.zeros_like(first_lo)], axis=1),
            np.concatenate([back_hi, back_hi], axis=1),
            np.concatenate([back_lo, np.zeros_like(back_lo)], axis=1),
        ]
    )
    seconds = np.concatenate([second_hi, second_lo], axis=2)
    turned = np.concatenate([turned_hi, turned_lo], axis=1)
    blocks = [plane[0], plane[1]]
    for part in (plane[2], plane[3]):
        blocks += [part[:, 0:256], part[:, 256:512]]
    blocks += [firsts.reshape(512, 256), seconds.reshape(1024, 256), turned.reshape(1024, 256)]
    ky, kx = plane_modes()
    sine_xy = 4 * np.sin(np.pi * ky / LY) ** 2 + 4 * np.sin(np.pi * kx / LX) ** 2
    sine_xy = np.repeat(sine_xy[:, None], 128, axis=1).astype(np.float32)
    tables = np.concatenate(blocks)
    waves = np.concatenate([base.reshape(512, 128), sine_xy])
    return np.resize(tables, (SPARE_ROWS, 256)), np.resize(waves, (SPARE_ROWS, 128))


def split(value):
    high = value.astype(BF16)
    return high, (value - high.astype(F32)).astype(BF16)


def fields_of(link):
    imag_sum = link(1, 0, 0) + link(1, 1, 1) + link(1, 2, 2)
    third = imag_sum * (2.0 / 3.0)
    return [
        link(0, 0, 1) - link(0, 1, 0),
        link(1, 0, 1) + link(1, 1, 0),
        link(0, 0, 2) - link(0, 2, 0),
        link(1, 0, 2) + link(1, 2, 0),
        link(0, 1, 2) - link(0, 2, 1),
        link(1, 1, 2) + link(1, 2, 1),
        2.0 * link(1, 0, 0) - third,
        2.0 * link(1, 1, 1) - third,
    ]


def inverse_root(value):
    guess = lax.rsqrt(value)
    return guess * (1.5 - 0.5 * value * guess * guess)


def cross_row(first, second):
    out = []
    for position in range(3):
        follow, beyond = (position + 1) % 3, (position + 2) % 3
        fr, fi = first[follow]
        gr, gi = first[beyond]
        sr, si = second[beyond]
        tr, ti = second[follow]
        real = fr * sr - fi * si - (gr * tr - gi * ti)
        imag = gr * ti + gi * tr - (fr * si + fi * sr)
        out.append((real, imag))
    return out


def gauge_of(x):
    a, b, c, d, e, f, d0, d1 = x
    n01 = a * a + b * b
    n02 = c * c + d * d
    n12 = e * e + f * f
    both = d0 + d1
    s01r = -both * b - (c * e + d * f)
    s01i = both * a - (d * e - c * f)
    s02r = d1 * d + (a * e - b * f)
    s02i = (a * f + b * e) - d1 * c
    s12r = d0 * f - (a * c + b * d)
    s12i = (b * c - a * d) - d0 * e
    r0 = [(1.0 - 0.5 * (d0 * d0 + n01 + n02), d0), (a + 0.5 * s01r, b + 0.5 * s01i), (c + 0.5 * s02r, d + 0.5 * s02i)]
    r1 = [(0.5 * s01r - a, b - 0.5 * s01i), (1.0 - 0.5 * (d1 * d1 + n01 + n12), d1), (e + 0.5 * s12r, f + 0.5 * s12i)]

    def unit(row):
        total = None
        for real, imag in row:
            term = real * real + imag * imag
            total = term if total is None else total + term
        scale = inverse_root(total)
        return [(real * scale, imag * scale) for real, imag in row]

    u0 = unit(r0)
    pr = pi = None
    for (ur, ui), (vr, vi) in zip(u0, r1):
        tr, ti = ur * vr + ui * vi, ur * vi - ui * vr
        pr = tr if pr is None else pr + tr
        pi = ti if pi is None else pi + ti
    v = [(vr - (pr * ur - pi * ui), vi - (pr * ui + pi * ur)) for (ur, ui), (vr, vi) in zip(u0, r1)]
    u1 = unit(v)
    return [u0, u1, cross_row(u0, u1)]


def rotated_link(left, link, right):
    rows = []
    for i in range(2):
        product = []
        for k in range(3):
            real = imag = None
            for m in range(3):
                lr, li = left[i][m]
                ur, ui = link(0, m, k), link(1, m, k)
                tr, ti = lr * ur - li * ui, lr * ui + li * ur
                real = tr if real is None else real + tr
                imag = ti if imag is None else imag + ti
            product.append((real, imag))
        row = []
        for j in range(3):
            real = imag = None
            for k in range(3):
                pr, pi = product[k]
                gr, gi = right[j][k]
                tr, ti = pr * gr + pi * gi, pi * gr - pr * gi
                real = tr if real is None else real + tr
                imag = ti if imag is None else imag + ti
            row.append((real, imag))
        rows.append(row)
    rows.append(cross_row(rows[0], rows[1]))
    return rows


def hop_count(offset):
    return sum(min(v, 4 - v) for v in offset[:3]) + 0.1 * offset[3]


OFFSETS = sorted(
    [
        (dx, dy, dz, dc)
        for dy in range(4)
        for dz in range(4)
        for dx in range(4)
        for dc in range(2)
        if dx + dy + dz + dc > 0
    ],
    key=lambda o: -hop_count(o),
)


def target(offset):
    ta = lax.axis_index("ta")
    gz = lax.axis_index("gz")
    y = (2 * (ta // 8) + gz % 2 + offset[1]) % 4
    to_ta = (y // 2) * 8 + (((ta // 2) % 4 + offset[0]) % 4) * 2 + (ta % 2 + offset[3]) % 2
    to_gz = ((gz // 2 + offset[2]) % 4) * 2 + y % 2
    return to_ta, to_gz


def kernel(
    links_hbm,
    tables_hbm,
    waves_hbm,
    out_hbm,
    links,
    tables,
    weight,
    sine,
    delta,
    along_y,
    along_z,
    exchange,
    smooth,
    gauge,
    ahead,
    link_out,
    link_in,
    link_last,
    edge_out,
    edge_in,
    edge,
    edge_modes,
    row_out,
    row_in,
    row_sem,
    table_sem,
    load_sem,
    store_sem,
    send_sem,
    recv_sem,
    edge_send_sem,
    edge_recv_sem,
):
    ta = lax.axis_index("ta")
    gz = lax.axis_index("gz")
    me = ta * NGZ + gz
    after = {"gz": (gz + 1) % NGZ}
    before = {"gz": (gz + NGZ - 1) % NGZ}

    barrier = pltpu.get_barrier_semaphore()
    loads = []
    for mu in (1, 0, 3, 2):
        for ct in range(8):
            copy = pltpu.make_async_copy(
                links_hbm.at[mu, :, :, :, 0, :, pl.ds(ct * 128, 128)],
                links.at[mu, :, :, :, pl.ds(ct * 8, 8), :],
                load_sem.at[mu],
            )
            copy.start()
    table_copies = [
        pltpu.make_async_copy(waves_hbm.at[pl.ds(0, 512)], weight, table_sem.at[0]),
        pltpu.make_async_copy(waves_hbm.at[pl.ds(pl.multiple_of(512 + me * 8, 8), 8)], sine, table_sem.at[1]),
        pltpu.make_async_copy(tables_hbm.at[pl.ds(0, 5632)], tables, table_sem.at[2]),
    ]
    for copy in table_copies:
        copy.start()
    for offset in OFFSETS:
        to_ta, to_gz = target(offset)
        pl.semaphore_signal(barrier, inc=1, device_id={"ta": to_ta, "gz": to_gz}, device_id_type=MESH)

    lane = lax.broadcasted_iota(jnp.int32, (8, 128), 1)
    first_x = lane % LX == 0
    last_x = lane % LX == LX - 1
    low_96 = lane < 96
    low_32 = lane < 32

    def tile_of(ref, mu, row):
        def link(part, i, k):
            return ref[mu, part, i, k, pl.ds(row, 8), :]

        return link

    def before_x(tile):
        return jnp.where(first_x, pltpu.roll(tile, 97, 1), pltpu.roll(tile, 1, 1))

    def after_x(tile):
        return jnp.where(last_x, pltpu.roll(tile, 31, 1), pltpu.roll(tile, 127, 1))

    def row_of(ct):
        return pl.multiple_of(ct * 8, 8)

    def wide_row(ct):
        return pl.multiple_of(ct * 16, 16)

    def load_wait(mu):
        whole = links.at[mu]
        pltpu.make_async_copy(whole, whole, load_sem.at[mu]).wait()

    def spread_fields(ct):
        row = row_of(ct)
        for f, value in enumerate(fields_of(tile_of(links, 1, row))):
            along_y[f, pl.ds(row, 8), :] = value
        wide = wide_row(ct)
        for f, value in enumerate(fields_of(tile_of(links, 2, row))):
            along_z[f, pl.ds(wide + 8, 8), :] = value

    top_row = lax.broadcasted_iota(jnp.int32, (8, 128), 0) == 0

    def edge_fields(ct):
        wide = wide_row(ct)
        column = pl.ds(pl.multiple_of(ct * 128, 128), 128)
        for f in range(8):
            tile = along_z[f, pl.ds(wide + 8, 8), :]
            edge[pl.ds(f * 8, 8), column] = jnp.where(top_row, pltpu.roll(tile, 1, 0), 0.0)
            edge[pl.ds(64 + f * 8, 8), column] = jnp.zeros((8, 128), F32)

    def gather_fields(ct):
        row = row_of(ct)
        previous = pl.multiple_of(((ct + 7) % 8) * 8, 8)
        column = pl.multiple_of(ct * 128, 128)
        in_x = fields_of(tile_of(links, 0, row))
        for f in range(8):
            total = before_x(in_x[f]) - in_x[f]
            here = along_y[f, pl.ds(row, 8), :]
            total += pltpu.roll(jnp.where(low_96, here, along_y[f, pl.ds(previous, 8), :]), 32, 1) - here
            delta[pl.ds(f * 8, 8), pl.ds(column, 128)] = total
        for f, value in enumerate(fields_of(tile_of(links, 3, row))):
            delta[pl.ds(64 + f * 8, 8), pl.ds(column, 128)] = value

    def gather_depth(ct):
        wide = wide_row(ct)
        column = pl.ds(pl.multiple_of(ct * 128, 128), 128)
        for f in range(8):
            delta[pl.ds(f * 8, 8), column] += along_z[f, pl.ds(wide + 7, 8), :] - along_z[f, pl.ds(wide + 8, 8), :]

    def each_tile(body):
        def step(ct, carry):
            body(ct)
            return carry

        lax.fori_loop(0, 8, step, 0)

    def exchange_start(slot, with_rows=False):
        source = exchange.at[slot]
        place = exchange.at[slot + 1]
        mine = pl.ds(pl.multiple_of(me * 8, 8), 8)
        pltpu.make_async_copy(source.at[mine], place.at[mine], recv_sem.at[slot // 2]).start()
        for offset in OFFSETS:
            to_ta, to_gz = target(offset)
            chunk = pl.ds(pl.multiple_of((to_ta * NGZ + to_gz) * 8, 8), 8)
            pltpu.make_async_remote_copy(
                source.at[chunk],
                place.at[mine],
                send_sem.at[slot // 2],
                recv_sem.at[slot // 2],
                device_id={"ta": to_ta, "gz": to_gz},
                device_id_type=MESH,
            ).start()
            if with_rows:
                pltpu.make_async_remote_copy(
                    row_out.at[to_ta * NGZ + to_gz],
                    row_in.at[me],
                    row_sem.at[0],
                    row_sem.at[1],
                    device_id={"ta": to_ta, "gz": to_gz},
                    device_id_type=MESH,
                ).start()
        if with_rows:
            pltpu.make_async_copy(row_out.at[me], row_in.at[me], row_sem.at[1]).start()

    def exchange_wait(slot):
        whole = exchange.at[slot + 1]
        pltpu.make_async_copy(whole, whole, recv_sem.at[slot // 2]).wait()

    def exchange_sent(slot):
        part = exchange.at[slot, pl.ds(0, 1016)]
        pltpu.make_async_copy(part, part, send_sem.at[slot // 2]).wait()

    def table(first, count, columns=256):
        return tables[first : first + count, 0:columns]

    def odd_table(part):
        first = 1024 + 1024 * part
        return jnp.concatenate([table(first, 512), table(first + 512, 512)], axis=1)

    def product_nt(left_hi, left_lo, right):
        high, low = split(right)
        both = jnp.concatenate([high, low], axis=0)
        dims = (((1,), (1,)), ((), ()))
        wide = lax.dot_general(left_hi, both, dims, preferred_element_type=F32)
        return wide[:, 0:128] + wide[:, 128:256] + lax.dot_general(left_lo, high, dims, preferred_element_type=F32)

    def plane_forward(source, place):
        x0, x1, x2, x3 = [source[:, a * 256 : (a + 1) * 256] for a in range(4)]
        p, m, q, n = x0 + x2, x0 - x2, x1 + x3, x1 - x3
        place[0:256, :] = product_nt(table(0, 256), table(512, 256), p + q)
        place[256:512, :] = product_nt(table(256, 256), table(768, 256), p - q)
        place[512:1024, :] = product_nt(odd_table(0), odd_table(1), jnp.concatenate([m, n], axis=1))

    def product_tn(left, right_hi, right_lo):
        turned_left = jnp.concatenate(
            [left[i * 128 : (i + 1) * 128, :].T for i in range(left.shape[0] // 128)], axis=1
        )
        high, low = split(turned_left)
        tall = jnp.dot(jnp.concatenate([high, low], axis=0), right_hi, preferred_element_type=F32)
        return tall[0:128] + tall[128:256] + jnp.dot(high, right_lo, preferred_element_type=F32)

    def plane_backward(slot):
        b0 = product_tn(exchange[slot, 0:256, :], table(0, 256), table(512, 256))
        b2 = product_tn(exchange[slot, 256:512, :], table(256, 256), table(768, 256))
        odd = product_tn(exchange[slot, 512:1024, :], odd_table(0), odd_table(1))
        c, s = odd[:, 0:256], odd[:, 256:512]
        plus, minus = b0 + b2, b0 - b2
        for a, value in enumerate((plus + c, minus + s, plus - c, minus - s)):
            for side in range(2):
                ct = 2 * a + side
                for sf in range(16):
                    smooth[sf, ct * 8 : ct * 8 + 8, :] = value[sf * 8 : sf * 8 + 8, side * 128 : side * 128 + 128]

    tall_lane = lax.broadcasted_iota(jnp.int32, (128, 128), 1)
    in_space = tall_lane < 64

    row_start = in_space & (tall_lane % 8 == 0)

    def pack_rows():
        total = edge_modes[pl.ds(0, 128, stride=8), :]
        for j in range(1, 8):
            total += pltpu.roll(edge_modes[pl.ds(j, 128, stride=8), :], j, 1)
        row_out[...] = total.reshape(128, 1, 128)

    def line_filter(slot, with_rows=False):
        parts = []
        if with_rows:
            rows = row_in[...].reshape(16, 8, 128)
            rows = pltpu.roll(rows, 1, 1).reshape(128, 128)
        for j in range(8):
            got = exchange[slot, pl.ds(j, 128, stride=8), :]
            late = jnp.concatenate([got[120:128], got[0:120]], axis=0)
            part = jnp.where(in_space, got, late - got)
            if with_rows:
                part += jnp.where(row_start, pltpu.roll(rows, 128 - j, 1) if j else rows, 0.0)
            parts.append(part)
        high, low = split(jnp.concatenate(parts, axis=1))
        stacked = jnp.concatenate([high, low], axis=0)
        lines = jnp.dot(table(3072, 128), stacked, preferred_element_type=F32)
        lines += jnp.dot(table(3200, 128, 128), high, preferred_element_type=F32)
        back = [[None] * 8 for _ in range(8)]
        for p in range(4):
            rows = []
            for j in range(8):
                rows.append(
                    jnp.concatenate(
                        [lines[p * 32 + h * 16 : p * 32 + h * 16 + 16, j * 128 : j * 128 + 128] for h in range(2)],
                        axis=1,
                    )
                )
            high, low = split(jnp.concatenate(rows, axis=0))
            wide = jnp.dot(high, table(3584 + 256 * p, 256), preferred_element_type=F32)
            modes = wide[:, 0:128] + wide[:, 128:256]
            modes += jnp.dot(low, table(3584 + 256 * p, 256, 128), preferred_element_type=F32)
            modes = modes * weight[p * 128 : p * 128 + 128, :]
            high, low = split(modes)
            turn_hi = table(4608 + 256 * p, 128)
            near = jnp.dot(high, turn_hi, preferred_element_type=F32)
            near += jnp.dot(low, turn_hi, preferred_element_type=F32)
            near += jnp.dot(high, table(4736 + 256 * p, 128), preferred_element_type=F32)
            for j in range(8):
                for h in range(2):
                    back[2 * p + h][j] = near[j * 16 : j * 16 + 16, h * 128 : h * 128 + 128]
        high, low = split(jnp.concatenate([jnp.concatenate(row, axis=1) for row in back], axis=0))
        stacked = jnp.concatenate([high, low], axis=0)
        sites = jnp.dot(table(3328, 128), stacked, preferred_element_type=F32)
        sites += jnp.dot(table(3456, 128, 128), high, preferred_element_type=F32)
        for j in range(8):
            here = sites[:, j * 128 : j * 128 + 128]
            early = jnp.concatenate([here[8:128], here[0:8]], axis=0)
            exchange[slot + 1, pl.ds(j, 128, stride=8), :] = jnp.where(in_space, here, early)

    def store_gauge(ref, row, matrix):
        for i in range(3):
            for k in range(3):
                for part in range(2):
                    ref[part, i, k, pl.ds(row, 8), :] = matrix[i][k][part]

    def load_gauge(ref, window):
        return [[(ref[0, i, k, window, :], ref[1, i, k, window, :]) for k in range(3)] for i in range(3)]

    def make_gauge(ct):
        row = row_of(ct)
        here = gauge_of([smooth[f, pl.ds(row, 8), :] for f in range(8)])
        store_gauge(gauge, wide_row(ct), here)
        store_gauge(gauge, pl.multiple_of(ct * 16 + 8, 8), here)
        store_gauge(ahead, row, gauge_of([smooth[8 + f, pl.ds(row, 8), :] for f in range(8)]))

    def store_link(mu, row, rows):
        for i in range(3):
            for k in range(3):
                for part in range(2):
                    links[mu, part, i, k, pl.ds(row, 8), :] = rows[i][k][part]

    def mapped(left, fn):
        return [[(fn(re), fn(im)) for re, im in row] for row in left]

    def rotate_xyt(ct):
        row = row_of(ct)
        left = load_gauge(gauge, pl.ds(wide_row(ct), 8))
        store_link(0, row, rotated_link(left, tile_of(links, 0, row), mapped(left, after_x)))
        following = load_gauge(gauge, pl.ds(pl.multiple_of(((ct + 1) % 8) * 16, 16), 8))
        right = [
            [
                tuple(pltpu.roll(jnp.where(low_32, following[i][k][part], left[i][k][part]), 96, 1) for part in range(2))
                for k in range(3)
            ]
            for i in range(3)
        ]
        store_link(1, row, rotated_link(left, tile_of(links, 1, row), right))
        store_link(3, row, rotated_link(left, tile_of(links, 3, row), load_gauge(ahead, pl.ds(row, 8))))

    def rotate_z(ct):
        row = row_of(ct)
        wide = wide_row(ct)
        left = load_gauge(gauge, pl.ds(wide, 8))
        right = load_gauge(gauge, pl.ds(wide + 1, 8))
        store_link(2, row, rotated_link(left, tile_of(links, 2, row), right))

    def edge_copy(way, device):
        return pltpu.make_async_remote_copy(
            edge_out.at[way], edge_in.at[way], edge_send_sem.at[way], edge_recv_sem.at[way], device_id=device,
            device_id_type=MESH,
        )

    load_wait(1)
    load_wait(2)
    for part in range(2):
        for i in range(3):
            for k in range(3):
                link_out[part, i, k] = links[2, part, i, k, pl.ds(7, 8, stride=8), :]
    each_tile(spread_fields)
    load_wait(0)
    load_wait(3)
    table_copies[0].wait()
    table_copies[1].wait()
    scale = 16.0 * 0.02 / (LX * LY * LZ * LT)
    for p in range(4):
        for j in range(8):
            total = weight[p * 128 + j * 16 : p * 128 + j * 16 + 16, :] + sine[j : j + 1, :]
            empty = total < 1e-6
            weight[p * 128 + j * 16 : p * 128 + j * 16 + 16, :] = jnp.where(empty, 0.0, scale / jnp.where(empty, 1.0, total))
    table_copies[2].wait()
    for f in range(8):
        along_z[f, pl.ds(7, 8, stride=16), :] = jnp.zeros((8, 128), F32)
    each_tile(gather_fields)
    each_tile(gather_depth)
    each_tile(edge_fields)
    plane_forward(edge, edge_modes)
    pack_rows()
    plane_forward(delta, exchange.at[0])
    pl.semaphore_wait(barrier, DEVICES - 1)
    exchange_start(0, True)
    link_copy = pltpu.make_async_remote_copy(
        link_out, link_in, edge_send_sem.at[4], edge_recv_sem.at[4], device_id=after, device_id_type=MESH
    )
    link_copy.start()

    for iteration in range(ITERS):
        last = iteration + 1 == ITERS
        slot = 4 * iteration
        if iteration > 0:
            each_tile(gather_depth)
            plane_forward(delta, exchange.at[slot])
            exchange_start(slot)
        else:
            pltpu.make_async_copy(row_in, row_in, row_sem.at[1]).wait()
        exchange_wait(slot)
        line_filter(slot + 1, iteration == 0)
        exchange_start(slot + 2)
        exchange_wait(slot + 2)
        plane_backward(slot + 3)
        high_way, low_way = 2 * iteration, 2 * iteration + 1
        for f in range(8):
            edge_out[high_way, f] = smooth[f, pl.ds(0, 8, stride=8), :]
        to_before = edge_copy(high_way, before)
        to_before.start()
        if not last:
            for f in range(8):
                edge_out[low_way, f] = smooth[f, pl.ds(7, 8, stride=8), :]
            to_after = edge_copy(low_way, after)
            to_after.start()
        each_tile(make_gauge)
        each_tile(rotate_xyt)
        if last:
            for mu in (0, 1, 3):
                for ct in range(8):
                    pltpu.make_async_copy(
                        links.at[mu, :, :, :, pl.ds(ct * 8, 8), :],
                        out_hbm.at[mu, :, :, :, 0, :, pl.ds(ct * 128, 128)],
                        store_sem.at[mu],
                    ).start()
        each_tile(rotate_z)
        if not last:
            each_tile(spread_fields)
            each_tile(gather_fields)
        to_before.wait_recv()
        halo = gauge_of([edge_in[high_way, f] for f in range(8)])
        left = load_gauge(gauge, pl.ds(7, 8, stride=16))
        before_last = link_out if iteration == 0 else link_last
        top = rotated_link(left, lambda part, i, k: before_last[part, i, k], halo)
        for part in range(2):
            for i in range(3):
                for k in range(3):
                    links[2, part, i, k, pl.ds(7, 8, stride=8), :] = top[i][k][part]
                    if not last:
                        link_last[part, i, k] = top[i][k][part]
        if last:
            for ct in range(8):
                pltpu.make_async_copy(
                    links.at[2, :, :, :, pl.ds(ct * 8, 8), :],
                    out_hbm.at[2, :, :, :, 0, :, pl.ds(ct * 128, 128)],
                    store_sem.at[2],
                ).start()
        else:
            for f, value in enumerate(fields_of(lambda part, i, k: top[i][k][part])):
                along_z[f, pl.ds(15, 8, stride=16), :] = value
            to_after.wait_recv()
            link_copy.wait_recv()
            left = gauge_of([edge_in[low_way, f] for f in range(8)])
            right = load_gauge(gauge, pl.ds(0, 8, stride=16))
            below = rotated_link(left, lambda part, i, k: link_in[part, i, k], right)
            for f, value in enumerate(fields_of(lambda part, i, k: below[i][k][part])):
                along_z[f, pl.ds(7, 8, stride=16), :] = value
            to_after.wait_send()
        to_before.wait_send()

    link_copy.wait_send()
    pltpu.make_async_copy(row_out.at[pl.ds(0, 127)], row_out.at[pl.ds(0, 127)], row_sem.at[0]).wait()
    for slot in range(0, 4 * ITERS, 2):
        exchange_sent(slot)
    for mu in range(4):
        whole = links.at[mu]
        pltpu.make_async_copy(whole, whole, store_sem.at[mu]).wait()


def on_device(gauge_links):
    operands = [jnp.asarray(table) for table in make_tables()]
    anywhere = pl.BlockSpec(memory_space=pl.ANY)
    scratch = [
        pltpu.VMEM((4, 2, 3, 3, 64, 128), F32),
        pltpu.VMEM((5632, 256), BF16),
        pltpu.VMEM((512, 128), F32),
        pltpu.VMEM((8, 128), F32),
        pltpu.VMEM((128, 1024), F32),
        pltpu.VMEM((8, 64, 128), F32),
        pltpu.VMEM((8, 128, 128), F32),
        pltpu.VMEM((4 * ITERS, 1024, 128), F32),
        pltpu.VMEM((16, 64, 128), F32),
        pltpu.VMEM((2, 3, 3, 128, 128), F32),
        pltpu.VMEM((2, 3, 3, 64, 128), F32),
        pltpu.VMEM((2, 3, 3, 8, 128), F32),
        pltpu.VMEM((2, 3, 3, 8, 128), F32),
        pltpu.VMEM((2, 3, 3, 8, 128), F32),
        pltpu.VMEM((4, 8, 8, 128), F32),
        pltpu.VMEM((4, 8, 8, 128), F32),
        pltpu.VMEM((128, 1024), F32),
        pltpu.VMEM((1024, 128), F32),
        pltpu.VMEM((128, 1, 128), F32),
        pltpu.VMEM((128, 1, 128), F32),
        pltpu.SemaphoreType.DMA((2,)),
        pltpu.SemaphoreType.DMA((3,)),
        pltpu.SemaphoreType.DMA((4,)),
        pltpu.SemaphoreType.DMA((4,)),
        pltpu.SemaphoreType.DMA((2 * ITERS,)),
        pltpu.SemaphoreType.DMA((2 * ITERS,)),
        pltpu.SemaphoreType.DMA((5,)),
        pltpu.SemaphoreType.DMA((5,)),
    ]
    return pl.pallas_call(
        kernel,
        out_shape=jax.ShapeDtypeStruct(gauge_links.shape, F32),
        in_specs=[anywhere] * (1 + len(operands)),
        out_specs=anywhere,
        scratch_shapes=scratch,
        compiler_params=pltpu.CompilerParams(
            collective_id=0, has_side_effects=True, vmem_limit_bytes=50 * 1024 * 1024
        ),
    )(gauge_links, *operands)


def solution(mesh):
    specs = P(None, None, None, None, "ta", "gz", None)
    return jax.shard_map(on_device, mesh=mesh, in_specs=(specs,), out_specs=specs, check_vma=False)
```
